256 devices in a mesh: section: 8 (over z_lo, x), expert: 32 (over y, z_hi, core).
Axes of the slice: x: 4, y: 4, z: 8 (z_hi: 4, z_lo: 2; z = z_hi * 2 + z_lo), core: 2. Of those that a mesh axis runs over, the one named last changes fastest.
Arguments:
- forward_batch: bfloat16 [8, 2048, 7168], P('section', 'expert'), may hold values from -6 to 6
- reverse_batch: bfloat16 [8, 2048, 7168], P('section', 'expert'), may hold values from -6 to 6
- norm_gain: float32 [8, 7168], P('section'), may hold values from 0.1 to 1.9
- routes: int32 [8, 2, 2, 2048, 1], P('section', None, None, 'expert'), may hold values from 0 to 7; in each aligned block of 64 rows (0 to 63, 64 to 127, ..., all dimensions but the last counted through in order) at most 8 rows name the same one
- gate_values: float32 [8, 2, 2, 2048, 1], P('section', None, None, 'expert'), may hold values from 0.2 to 1
- up_weight: bfloat16 [8, 32, 7168, 256], P('section', 'expert'), may hold values from -0.0625 to 0.0625
- down_weight: bfloat16 [8, 32, 256, 7168], P('section', 'expert'), may hold values from -0.1875 to 0.1875
Outputs:
- forward_out: bfloat16 [8, 2048, 7168], P('section', 'expert')
- reverse_out: bfloat16 [8, 2048, 7168], P('section', 'expert')
The draws below stay inside these ranges and needn't reach their ends.
Inputs may be any that keep to these rules, and one draw needn't show every extreme that they name: `routes`: each token names exactly one expert; for each section, direction and step, the 64 tokens of one device name every expert exactly 8 times.
All inputs are finite; a program needn't handle non-finite values.
Results may differ from the reference program's by a relative error of at most 0.006.
Values may be sent and summed in bfloat16 or wider, within the bound.
No kernel may reach another device: no remote copies, remote signals or barrier semaphores. Data moves between devices by JAX's collectives and lax.ppermute only.
A program may use at most 128 MiB of HBM per device.

```python
import math
import jax
import jax.numpy as jnp
import numpy as np
from jax import lax

D = 7168
EXP_FF = 1024
SPLIT = 4
SLICE_FF = 256
TOK_DEV = 64
TOP = 1
STEPS = 2
SECTIONS = 8
EXPERTS = 8
SLICES = 32
CAP = 8
TOKENS = 2048
N_EXPERT = 32


def shard_levels(key, shape, pieces, low, high):
    loudness = 1.0
    for axis_at, parts in pieces:
        steps = jax.random.uniform(jax.random.fold_in(jax.random.fold_in(key, 6), axis_at), (parts,), jnp.float32, low / len(pieces), high / len(pieces))
        loudness = loudness * jnp.repeat(jnp.exp(steps), shape[axis_at] // parts).reshape((-1,) + (1,) * (len(shape) - 1 - axis_at))
    return loudness


def routed_block(own_key, own, number, rows, number_of, top, reach, lean):
    order = jax.random.permutation(own_key, number_of)
    crowded, ordinary = load_shares(number_of, rows * top, reach, lean, True), load_shares(number_of, rows * top, reach, lean, False)
    places = jnp.arange(number_of)

    def named(tallies, offset_by):
        used = int((tallies > 0).sum())
        fixed = max(1, used // 4)
        shifted = fixed + (places - fixed + offset_by * (used - fixed)) % max(1, number_of - fixed)
        return jnp.zeros((number_of,), jnp.int32).at[order[jnp.where(places < fixed, places, shifted)]].set(jnp.asarray(tallies, jnp.int32))

    tallies = jnp.where(number % 4 == 0, named(crowded, number // 4), named(ordinary, number - number // 4 - 1))
    mixed = jax.random.permutation(jax.random.fold_in(own, 3), number_of)
    donor, sink = mixed[0:number_of // 2 * 2:2], mixed[1:number_of // 2 * 2:2]
    room = jnp.minimum(tallies[donor] - 1, reach - tallies[sink]) // 2
    room = jnp.where((donor == order[0]) | (sink == order[0]) | (tallies[sink] == 0), 0, jnp.maximum(room, 0))
    shifted = jax.random.randint(jax.random.fold_in(own, 4), (number_of // 2,), 0, 1 << 20) % (room + 1)
    tallies = tallies.at[donor].add(-shifted).at[sink].add(shifted)
    members = jnp.searchsorted(jnp.cumsum(tallies), jnp.arange(rows * top), side="right").astype(jnp.int32)
    listing = members.reshape(top, rows).T
    listing = listing[jax.random.permutation(jax.random.fold_in(own, 1), rows)]
    offset_by = jax.random.randint(jax.random.fold_in(own, 2), (rows, 1), 0, top)
    return jnp.take_along_axis(listing, (jnp.arange(top)[None, :] + offset_by) % top, axis=1)


def load_shares(number_of, total, reach, skew, full):
    portions = [(1 << 20) // math.isqrt(grade ** skew) + 1 for grade in range(1, number_of + 1)]
    largest = reach if full else min(reach, max(-(-total // number_of), total * portions[0] // sum(portions)))
    least = 1 if total - largest >= number_of - 1 else 0
    holding, rest = [largest] + [least] * (number_of - 1), total - largest - least * (number_of - 1)
    while rest > 0:
        free = [i for i in range(1, number_of) if holding[i] < largest] or [i for i in range(1, number_of) if holding[i] < reach]
        pool, budget = sum([portions[i] for i in free]), rest
        for i in free:
            addition = min(reach - holding[i], max(1, budget * portions[i] // pool), rest)
            holding[i] = holding[i] + addition
            rest = rest - addition
    return np.array(holding)


def gaussian(key, extent, scale, reach, pieces=(), kind=jnp.bfloat16):
    level = shard_levels(key, extent, pieces, -0.22, 0.18) if pieces else 1.0
    drawn = jax.random.normal(key, extent, jnp.float32) * scale * level
    return jnp.minimum(jnp.maximum(drawn, -reach), reach).astype(kind)


def setup_inputs(seed: int = 0) -> dict:
    key_list = jax.random.split(jax.random.key(seed), 8)
    forward_batch = gaussian(key_list[0], (SECTIONS, TOKENS, D), 1.0, 6.0, ((0, 8), (1, 32)))
    reverse_batch = gaussian(key_list[1], (SECTIONS, TOKENS, D), 1.0, 6.0, ((0, 8), (1, 32)))
    norm_gain = jnp.clip(1.0 + 0.18 * jax.random.normal(key_list[2], (SECTIONS, D), jnp.float32), 0.1, 1.9)
    routes_keys = jax.random.split(jax.random.fold_in(key_list[3], 1), SECTIONS * 2 * STEPS * TOKENS // TOK_DEV)
    routes_turns = jax.random.permutation(jax.random.fold_in(key_list[3], 3), SECTIONS * 2 * STEPS * TOKENS // TOK_DEV)
    routes = jax.vmap(lambda own, number: routed_block(jax.random.fold_in(key_list[3], 2), own, number, TOK_DEV, EXPERTS, TOP, CAP, 0))(routes_keys, routes_turns).reshape((SECTIONS, 2, STEPS, TOKENS, TOP))
    gate_values = jnp.clip(jnp.exp(math.log(1.0) - 1.609438 * jax.random.uniform(key_list[4], (SECTIONS, 2, STEPS, TOKENS, TOP), jnp.float32) ** shard_levels(key_list[4], (SECTIONS, 2, STEPS, TOKENS, TOP), ((0, 8), (3, 32)), -0.2, 0.2)), 0.2, 1.0)
    up_weight = gaussian(key_list[5], (SECTIONS, SLICES, D, SLICE_FF), D ** -0.5, 0.0625, ((0, 8), (1, 32)))
    down_weight = gaussian(key_list[6], (SECTIONS, SLICES, SLICE_FF, D), EXP_FF ** -0.5, 0.1875, ((0, 8), (1, 32)))
    return dict(forward_batch=forward_batch, reverse_batch=reverse_batch, norm_gain=norm_gain, routes=routes, gate_values=gate_values, up_weight=up_weight, down_weight=down_weight)


epsilon = 1e-06

def slot_matrix(route_flat, experts):
    chosen = (route_flat[:, None] == jnp.arange(experts, dtype=jnp.int32)[None, :]).astype(jnp.int32)
    before = jnp.cumsum(chosen, axis=0) - chosen
    position = lax.optimization_barrier(jnp.sum(chosen * before, axis=1))
    target = route_flat * CAP + position
    return (target[:, None] == jnp.arange(experts * CAP, dtype=jnp.int32)[None, :]).astype(jnp.float32)

def run_expert(arrived, up_slices, down_slices):
    total = jnp.zeros((arrived.shape[0], D), jnp.float32)
    for quarter in range(SPLIT):
        up_values = jnp.dot(arrived, up_slices[quarter], preferred_element_type=jnp.float32)
        activated = jax.nn.silu(up_values).astype(jnp.bfloat16)
        partial_value = jnp.dot(activated, down_slices[quarter], preferred_element_type=jnp.float32).astype(jnp.bfloat16)
        partial_value = lax.optimization_barrier(partial_value)
        total = total + partial_value.astype(jnp.float32)
    return total.astype(jnp.bfloat16)

def routed_layer(current, norm_scale, route, weighting, up_matrix, down_matrix):
    up_grouped = up_matrix.reshape(EXPERTS, SPLIT, D, SLICE_FF)
    down_grouped = down_matrix.reshape(EXPERTS, SPLIT, SLICE_FF, D)
    as_float = current.astype(jnp.float32)
    normed = (as_float * lax.rsqrt(lax.optimization_barrier(jnp.mean(as_float * as_float, axis=-1, keepdims=True)) + epsilon) * norm_scale).astype(jnp.bfloat16)
    token_rows = jnp.repeat(normed, TOP, axis=0).reshape(N_EXPERT, TOK_DEV * TOP, D)
    tables = jax.vmap(lambda packed: slot_matrix(packed, EXPERTS))(route.reshape(N_EXPERT, TOK_DEV * TOP))
    sending = jnp.einsum('nas,nad->nsd', tables, token_rows.astype(jnp.float32)).astype(jnp.bfloat16)
    sending = sending.reshape(N_EXPERT, EXPERTS, CAP, D).transpose(1, 0, 2, 3).reshape(EXPERTS, N_EXPERT * CAP, D)
    produced = lax.map(lambda packed: run_expert(packed[0], packed[1], packed[2]), (sending, up_grouped, down_grouped))
    produced = produced.reshape(EXPERTS, N_EXPERT, CAP, D).transpose(1, 0, 2, 3).reshape(N_EXPERT, EXPERTS * CAP, D)
    returned = jnp.einsum('nas,nsd->nad', tables, produced.astype(jnp.float32))
    mixed = lax.optimization_barrier(jnp.sum(returned.reshape(TOKENS, TOP, D) * weighting[:, :, None], axis=1))
    return (as_float + mixed).astype(jnp.bfloat16)

def reference(forward_batch, reverse_batch, norm_gain, routes, gate_values, up_weight, down_weight):
    states = [forward_batch, reverse_batch]
    for moment in range(STEPS):
        for course in range(2):
            states[course] = lax.map(lambda packed: routed_layer(packed[0], packed[1], packed[2], packed[3], packed[4], packed[5]), (states[course], norm_gain, routes[:, course, moment], gate_values[:, course, moment], up_weight, down_weight))
        if moment + 1 < STEPS:
            states[0] = jnp.roll(states[0], 1, axis=0)
            states[1] = jnp.roll(states[1], -1, axis=0)
    return (states[0], states[1])
```

```python
import jax
import jax.numpy as jnp
from jax import lax
from jax.sharding import PartitionSpec as P

SPLIT = 4
STEPS = 2
CORES = 2
HALVES = SPLIT // CORES

epsilon = 1e-06


def passed_along(array, axis, by):
    size = lax.axis_size(axis)
    return lax.ppermute(array, axis, [(i, (i + by) % size) for i in range(size)])


def swapped(array):
    size = lax.axis_size("expert")
    return lax.ppermute(array, "expert", [(i, i ^ 1) for i in range(size)])


def slot_matrix(route_flat, experts, capacity):
    chosen = (route_flat[:, None] == jnp.arange(experts, dtype=jnp.int32)[None, :]).astype(
        jnp.int32
    )
    before = jnp.cumsum(chosen, axis=0) - chosen
    position = jnp.sum(chosen * before, axis=1)
    target = route_flat * capacity + position
    return (target[:, None] == jnp.arange(experts * capacity, dtype=jnp.int32)[None, :]).astype(
        jnp.bfloat16
    )


def prepare(current, norm_scale, slot_table, experts, capacity):
    width = current.shape[1]
    as_float = current.astype(jnp.float32)
    normed = (
        as_float
        * lax.rsqrt(jnp.mean(as_float * as_float, axis=-1, keepdims=True) + epsilon)
        * norm_scale
    ).astype(jnp.bfloat16)
    rows = jnp.einsum(
        "as,ad->sd", slot_table, normed, preferred_element_type=jnp.float32
    ).astype(jnp.bfloat16)
    part = width // CORES
    rows = rows.reshape(experts, capacity, CORES, part).transpose(0, 2, 1, 3)
    copies = jnp.broadcast_to(rows[:, None], (experts, HALVES, CORES, capacity, part))
    return copies.reshape(experts * SPLIT, capacity, part)


def exchange(blocks):
    return lax.all_to_all(blocks, "expert", split_axis=0, concat_axis=0, tiled=True)


def expert_rows(arrived, up_matrix, down_matrix):
    layout = arrived.shape
    hidden = up_matrix.shape[1] // CORES
    sums = jnp.dot(arrived.reshape(-1, layout[-1]), up_matrix, preferred_element_type=jnp.float32)
    theirs = swapped(sums)
    total = sums + jnp.concatenate([theirs[:, hidden:], theirs[:, :hidden]], axis=1)
    activated = jax.nn.silu(total).astype(jnp.bfloat16)
    partial = jnp.dot(activated, down_matrix, preferred_element_type=jnp.float32)
    return partial.astype(jnp.bfloat16).reshape(layout)


def finish(current, slot_table, returned, weighting, experts, capacity):
    tokens, width = current.shape
    part = width // CORES
    summed = jnp.sum(
        returned.reshape(experts, HALVES, CORES, capacity, part).astype(jnp.float32), axis=1
    ).astype(jnp.bfloat16)
    produced = summed.transpose(0, 2, 1, 3).reshape(experts * capacity, width)
    gathered = jnp.einsum("as,sd->ad", slot_table, produced, preferred_element_type=jnp.float32)
    return (current.astype(jnp.float32) + gathered * weighting).astype(jnp.bfloat16)


def per_device(
    forward_batch, reverse_batch, norm_gain, routes, gate_values, up_weight, down_weight
):
    devices = lax.axis_size("expert")
    experts = devices // SPLIT
    states = [forward_batch[0], reverse_batch[0]]
    tokens, width = states[0].shape
    capacity = tokens // experts
    norm_scale = norm_gain[0]
    part = width // CORES

    core = lax.axis_index("expert") % CORES
    up_own, down_own = up_weight[0, 0], down_weight[0, 0]
    up_kept = lax.dynamic_slice_in_dim(up_own, core * part, part, 0)
    up_given = lax.dynamic_slice_in_dim(up_own, (1 - core) * part, part, 0)
    down_kept = lax.dynamic_slice_in_dim(down_own, core * part, part, 1)
    down_given = lax.dynamic_slice_in_dim(down_own, (1 - core) * part, part, 1)
    up_matrix = jnp.concatenate([up_kept, swapped(up_given)], axis=1)
    down_matrix = jnp.concatenate([down_kept, swapped(down_given)], axis=0)

    tables = [
        [slot_matrix(routes[0, c, t].reshape(-1), experts, capacity) for c in range(2)]
        for t in range(STEPS)
    ]
    for moment in range(STEPS):
        sending = [
            prepare(states[c], norm_scale, tables[moment][c], experts, capacity) for c in range(2)
        ]
        arrived = [exchange(sending[c]) for c in range(2)]
        results = [expert_rows(arrived[c], up_matrix, down_matrix) for c in range(2)]
        returned = [exchange(results[c]) for c in range(2)]
        states = [
            finish(
                states[c],
                tables[moment][c],
                returned[c],
                gate_values[0, c, moment],
                experts,
                capacity,
            )
            for c in range(2)
        ]
        if moment + 1 < STEPS:
            states[0] = passed_along(states[0], "section", 1)
            states[1] = passed_along(states[1], "section", -1)
    return (states[0][None], states[1][None])


def solution(mesh):
    return jax.shard_map(
        per_device,
        mesh=mesh,
        in_specs=(
            P("section", "expert", None),
            P("section", "expert", None),
            P("section", None),
            P("section", None, None, "expert", None),
            P("section", None, None, "expert", None),
            P("section", "expert", None, None),
            P("section", "expert", None, None),
        ),
        out_specs=(P("section", "expert", None), P("section", "expert", None)),
        check_vma=False,
    )
```

```python
import functools

import jax
import jax.numpy as jnp
from jax import lax
from jax.experimental import pallas as pl
from jax.experimental.pallas import tpu as pltpu
from jax.sharding import PartitionSpec as P

SPLIT = 4
STEPS = 2
CORES = 2
HALVES = SPLIT // CORES
COURSES = 2
TILE = 512
VMEM_BYTES = 20 * 1024 * 1024

epsilon = 1e-06

F32 = jnp.float32
BF16 = jnp.bfloat16


def passed_along(array, axis, by):
    size = lax.axis_size(axis)
    return lax.ppermute(array, axis, [(i, (i + by) % size) for i in range(size)])


def across_cores(array):
    size = lax.axis_size("expert")
    return lax.ppermute(array, "expert", [(i, i ^ 1) for i in range(size)])


def exchange(blocks):
    return lax.all_to_all(blocks, "expert", split_axis=0, concat_axis=0, tiled=True)


def kernel_call(body, shape, dtype, *operands):
    return pl.pallas_call(
        body,
        out_shape=jax.ShapeDtypeStruct(shape, dtype),
        in_specs=[pl.BlockSpec(memory_space=pltpu.VMEM)] * len(operands),
        out_specs=pl.BlockSpec(memory_space=pltpu.VMEM),
        compiler_params=pltpu.CompilerParams(vmem_limit_bytes=VMEM_BYTES),
    )(*operands)


def tiles(width):
    step = TILE if width % TILE == 0 else width
    return [(start, start + step) for start in range(0, width, step)]


def iota(shape, axis):
    return lax.broadcasted_iota(jnp.int32, shape, axis)


def slots_by_tokens(route, experts, capacity):
    tokens = route.shape[1]
    chosen = (iota((experts, tokens), 0) == route).astype(F32)
    earlier = (iota((tokens, tokens), 0) < iota((tokens, tokens), 1)).astype(BF16)
    before = jnp.dot(chosen.astype(BF16), earlier, preferred_element_type=F32)
    position = jnp.sum(chosen * before, axis=0, keepdims=True).astype(jnp.int32)
    return (iota((experts * capacity, tokens), 0) == route * capacity + position).astype(BF16)


def tokens_by_slots(route, experts, capacity):
    tokens = route.shape[0]
    chosen = (iota((tokens, experts), 1) == route).astype(F32)
    earlier = (iota((tokens, tokens), 1) < iota((tokens, tokens), 0)).astype(BF16)
    before = jnp.dot(earlier, chosen.astype(BF16), preferred_element_type=F32)
    position = jnp.sum(chosen * before, axis=1, keepdims=True).astype(jnp.int32)
    return (iota((tokens, experts * capacity), 1) == route * capacity + position).astype(BF16)


def prepare_body(experts, capacity, first, second, gain, routes, out):
    width = first.shape[1]
    part = width // CORES
    states = (first, second)
    scales, tables = [], []
    for course, state in enumerate(states):
        total = jnp.zeros((state.shape[0], 1), F32)
        for low, high in tiles(width):
            piece = state[:, low:high].astype(F32)
            total = total + jnp.sum(piece * piece, axis=1, keepdims=True)
        scales.append(lax.rsqrt(total / width + epsilon))
        tables.append(slots_by_tokens(routes[course : course + 1, :], experts, capacity))
    for core in range(CORES):
        for low, high in tiles(part):
            columns = slice(core * part + low, core * part + high)
            rows = []
            for state, scale, table in zip(states, scales, tables):
                normed = (state[:, columns].astype(F32) * scale * gain[:, columns]).astype(BF16)
                rows.append(jnp.dot(table, normed, preferred_element_type=F32))
            for e in range(experts):
                span = slice(e * capacity, (e + 1) * capacity)
                block = jnp.concatenate([r[span] for r in rows], axis=0).astype(BF16)
                for half in range(HALVES):
                    out[e * SPLIT + half * CORES + core, :, low:high] = block


def up_body(rows, kept, got, out):
    hidden = kept.shape[1]
    out[:, :hidden] = jnp.dot(rows[...], kept[...], preferred_element_type=F32)
    out[:, hidden:] = jnp.dot(rows[...], got[...], preferred_element_type=F32)


def down_body(mine, theirs, kept, got, out):
    hidden = kept.shape[0]
    first = jax.nn.silu(mine[:, :hidden] + theirs[:, hidden:]).astype(BF16)
    second = jax.nn.silu(mine[:, hidden:] + theirs[:, :hidden]).astype(BF16)
    for low, high in tiles(kept.shape[1]):
        total = jnp.dot(first, kept[:, low:high], preferred_element_type=F32)
        total = total + jnp.dot(second, got[:, low:high], preferred_element_type=F32)
        out[:, low:high] = total.astype(out.dtype)


def finish_body(experts, capacity, course, state, returned, route, gate, out):
    width = state.shape[1]
    part = width // CORES
    table = tokens_by_slots(route[...], experts, capacity)
    span = slice(course * capacity, (course + 1) * capacity)
    for core in range(CORES):
        for low, high in tiles(part):
            columns = slice(core * part + low, core * part + high)
            produced = []
            for e in range(experts):
                blocks = [
                    returned[e * SPLIT + half * CORES + core, :, low:high].astype(F32)[span]
                    for half in range(HALVES)
                ]
                produced.append(sum(blocks))
            produced = jnp.concatenate(produced, axis=0).astype(BF16)
            gathered = jnp.dot(table, produced, preferred_element_type=F32)
            out[:, columns] = (state[:, columns].astype(F32) + gathered * gate[...]).astype(BF16)


def per_device(
    forward_batch, reverse_batch, norm_gain, routes, gate_values, up_weight, down_weight
):
    devices = lax.axis_size("expert")
    experts = devices // SPLIT
    states = [forward_batch[0], reverse_batch[0]]
    tokens, width = states[0].shape
    capacity = tokens // experts
    part = width // CORES
    hidden = up_weight.shape[-1]
    block = (devices, COURSES * capacity, part)

    core = lax.axis_index("expert") % CORES
    up_own, down_own = up_weight[0, 0], down_weight[0, 0]
    up_got = across_cores(lax.dynamic_slice_in_dim(up_own, (1 - core) * part, part, 0))
    down_got = across_cores(lax.dynamic_slice_in_dim(down_own, (1 - core) * part, part, 1))
    up_kept = lax.dynamic_slice_in_dim(up_own, core * part, part, 0)
    down_kept = lax.dynamic_slice_in_dim(down_own, core * part, part, 1)

    for t in range(STEPS):
        sending = kernel_call(
            functools.partial(prepare_body, experts, capacity),
            block,
            BF16,
            *states,
            norm_gain,
            routes[0, :, t, :, 0],
        )
        rows = exchange(sending).reshape(-1, part)
        sums = kernel_call(up_body, (rows.shape[0], hidden * CORES), F32, rows, up_kept, up_got)
        partial = kernel_call(
            down_body, rows.shape, BF16, sums, across_cores(sums), down_kept, down_got
        )
        returned = exchange(partial.reshape(block))
        for c in range(COURSES):
            states[c] = kernel_call(
                functools.partial(finish_body, experts, capacity, c),
                (tokens, width),
                BF16,
                states[c],
                returned,
                routes[0, c, t],
                gate_values[0, c, t],
            )
            if t + 1 < STEPS:
                states[c] = passed_along(states[c], "section", 1 - 2 * c)
    return (states[0][None], states[1][None])


def solution(mesh):
    return jax.shard_map(
        per_device,
        mesh=mesh,
        in_specs=(
            P("section", "expert", None),
            P("section", "expert", None),
            P("section", None),
            P("section", None, None, "expert", None),
            P("section", None, None, "expert", None),
            P("section", "expert", None, None),
            P("section", "expert", None, None),
        ),
        out_specs=(P("section", "expert", None), P("section", "expert", None)),
        check_vma=False,
    )
```

```python
import functools

import jax
import jax.numpy as jnp
from jax import lax
from jax.experimental import pallas as pl
from jax.experimental.pallas import tpu as pltpu
from jax.sharding import PartitionSpec as P

SPLIT = 4
STEPS = 2
CORES = 2
HALVES = SPLIT // CORES
COURSES = 2
TILE = 512
SMALL = 20 * 1024 * 1024
LARGE = 56 * 1024 * 1024

epsilon = 1e-06

F32 = jnp.float32
BF16 = jnp.bfloat16


def passed_along(array, axis, by):
    size = lax.axis_size(axis)
    return lax.ppermute(array, axis, [(i, (i + by) % size) for i in range(size)])


def across_cores(array):
    size = lax.axis_size("expert")
    return lax.ppermute(array, "expert", [(i, i ^ 1) for i in range(size)])


def exchange(blocks):
    return lax.all_to_all(blocks, "expert", split_axis=0, concat_axis=0, tiled=True)


def params(limit):
    return pltpu.CompilerParams(vmem_limit_bytes=limit)


def tiles(width):
    step = TILE if width % TILE == 0 else width
    return [(start, start + step) for start in range(0, width, step)]


def iota(shape, axis):
    return lax.broadcasted_iota(jnp.int32, shape, axis)


def slots_by_tokens(route, experts, capacity):
    tokens = route.shape[1]
    chosen = (iota((experts, tokens), 0) == route).astype(F32)
    earlier = (iota((tokens, tokens), 0) < iota((tokens, tokens), 1)).astype(BF16)
    before = jnp.dot(chosen.astype(BF16), earlier, preferred_element_type=F32)
    position = jnp.sum(chosen * before, axis=0, keepdims=True).astype(jnp.int32)
    return (iota((experts * capacity, tokens), 0) == route * capacity + position).astype(BF16)


def column(line):
    size = line.shape[1]
    same = iota((size, size), 0) == iota((size, size), 1)
    return jnp.sum(jnp.where(same, line, jnp.zeros_like(line)), axis=1, keepdims=True)


def tokens_by_slots(route, experts, capacity):
    tokens = route.shape[0]
    chosen = (iota((tokens, experts), 1) == route).astype(F32)
    earlier = (iota((tokens, tokens), 1) < iota((tokens, tokens), 0)).astype(BF16)
    before = jnp.dot(earlier, chosen.astype(BF16), preferred_element_type=F32)
    position = jnp.sum(chosen * before, axis=1, keepdims=True).astype(jnp.int32)
    return (iota((tokens, experts * capacity), 1) == route * capacity + position).astype(BF16)


def prepare_body(experts, capacity, moment, first, second, gain, routes, out, slotted, sems):
    width = first.shape[1]
    part = width // CORES
    states = (first, second)
    scales, tables = [], []
    for course, state in enumerate(states):
        total = jnp.zeros((state.shape[0], 1), F32)
        for low, high in tiles(width):
            piece = state[:, low:high].astype(F32)
            total = total + jnp.sum(piece * piece, axis=1, keepdims=True)
        scales.append(lax.rsqrt(total / width + epsilon))
        tables.append(slots_by_tokens(routes[course, moment], experts, capacity))
    copies = []
    for core in range(CORES):
        for low, high in tiles(part):
            columns = slice(core * part + low, core * part + high)
            rows = []
            for state, scale, table in zip(states, scales, tables):
                normed = (state[:, columns].astype(F32) * scale * gain[:, columns]).astype(BF16)
                rows.append(jnp.dot(table, normed, preferred_element_type=F32))
            for e in range(experts):
                span = slice(e * capacity, (e + 1) * capacity)
                block = jnp.concatenate([r[span] for r in rows], axis=0).astype(BF16)
                slotted[core, e, :, low:high] = block
        for half in range(HALVES):
            copy = pltpu.make_async_copy(
                slotted.at[core], out.at[:, half, core], sems.at[core, half]
            )
            copy.start()
            copies.append(copy)
    for copy in copies:
        copy.wait()


def prepare(states, gain, routes, experts, capacity, moment, limit):
    part = states[0].shape[1] // CORES
    rows = COURSES * capacity
    return pl.pallas_call(
        functools.partial(prepare_body, experts, capacity, moment),
        out_shape=jax.ShapeDtypeStruct((experts, HALVES, CORES, rows, part), BF16),
        in_specs=[pl.BlockSpec(memory_space=pltpu.VMEM)] * 4,
        out_specs=pl.BlockSpec(memory_space=pl.ANY),
        scratch_shapes=[
            pltpu.VMEM((CORES, experts, rows, part), BF16),
            pltpu.SemaphoreType.DMA((CORES, HALVES)),
        ],
        compiler_params=params(limit),
    )(*states, gain, routes)


def started(pairs, sems):
    copies = [pltpu.make_async_copy(*pair, sems.at[i]) for i, pair in enumerate(pairs)]
    for copy in copies:
        copy.start()
    return copies


def streamed_up_body(rows, kept, got, out, rows_held, kept_held, got_held, sems):
    hidden = kept.shape[1]
    bounds = tiles(rows.shape[1])
    pairs = []
    for low, high in bounds:
        span = slice(low, high)
        pairs.append((kept.at[span], kept_held.at[span]))
        pairs.append((got.at[span], got_held.at[span]))
        pairs.append((rows.at[:, span], rows_held.at[:, span]))
    copies = started(pairs, sems)
    for i, (low, high) in enumerate(bounds):
        for copy in copies[3 * i : 3 * i + 3]:
            copy.wait()
        piece = rows_held[:, low:high]
        mine = jnp.dot(piece, kept_held[low:high], preferred_element_type=F32)
        other = jnp.dot(piece, got_held[low:high], preferred_element_type=F32)
        if i == 0:
            out[:, :hidden] = mine
            out[:, hidden:] = other
        else:
            out[:, :hidden] += mine
            out[:, hidden:] += other


def up_body(rows, kept, got, out):
    hidden = kept.shape[1]
    out[:, :hidden] = jnp.dot(rows[...], kept[...], preferred_element_type=F32)
    out[:, hidden:] = jnp.dot(rows[...], got[...], preferred_element_type=F32)


def up(rows, kept, got, streamed):
    count, part = rows.shape
    scratch = [
        pltpu.VMEM(rows.shape, BF16),
        pltpu.VMEM(kept.shape, BF16),
        pltpu.VMEM(got.shape, BF16),
        pltpu.SemaphoreType.DMA((3 * len(tiles(part)),)),
    ]
    return pl.pallas_call(
        streamed_up_body if streamed else up_body,
        out_shape=jax.ShapeDtypeStruct((count, CORES * kept.shape[1]), F32),
        in_specs=[pl.BlockSpec(memory_space=pl.ANY if streamed else pltpu.VMEM)] * 3,
        out_specs=pl.BlockSpec(memory_space=pltpu.VMEM),
        scratch_shapes=scratch if streamed else [],
        compiler_params=params(LARGE if streamed else SMALL),
    )(rows, kept, got)


def down_body(mine, theirs, kept, got, out):
    hidden = kept.shape[0]
    first = jax.nn.silu(mine[:, :hidden] + theirs[:, hidden:]).astype(BF16)
    second = jax.nn.silu(mine[:, hidden:] + theirs[:, :hidden]).astype(BF16)
    for low, high in tiles(kept.shape[1]):
        total = jnp.dot(first, kept[:, low:high], preferred_element_type=F32)
        total = total + jnp.dot(second, got[:, low:high], preferred_element_type=F32)
        out[:, low:high] = total.astype(out.dtype)


def down(mine, theirs, kept, got):
    return pl.pallas_call(
        down_body,
        out_shape=jax.ShapeDtypeStruct((mine.shape[0], kept.shape[1]), BF16),
        in_specs=[pl.BlockSpec(memory_space=pltpu.VMEM)] * 4,
        out_specs=pl.BlockSpec(memory_space=pltpu.VMEM),
        compiler_params=params(SMALL),
    )(mine, theirs, kept, got)


def finish_body(
    capacity, moment, first, second, returned, routes, gates, new_first, new_second, held, sems
):
    experts = returned.shape[0]
    part = returned.shape[-1]
    step = part // 2
    spans = [(core, low) for core in range(CORES) for low in (0, step)]
    copies = started(
        [
            (
                returned.at[:, :, core, :, low : low + step],
                held.at[:, :, core, :, low : low + step],
            )
            for core, low in spans
        ],
        sems,
    )
    chosen = [column(routes[course, moment]) for course in range(COURSES)]
    tables = [tokens_by_slots(route, experts, capacity) for route in chosen]
    scales = [column(gates[course, moment]) for course in range(COURSES)]
    for copy, (core, start) in zip(copies, spans):
        copy.wait()
        for low in range(start, start + step, TILE // 2):
            high = low + TILE // 2
            summed = [
                held[e, 0, core, :, low:high].astype(F32)
                + held[e, 1, core, :, low:high].astype(F32)
                for e in range(experts)
            ]
            columns = slice(core * part + low, core * part + high)
            for course, (state, new) in enumerate(((first, new_first), (second, new_second))):
                span = slice(course * capacity, (course + 1) * capacity)
                produced = jnp.concatenate([block[span] for block in summed], axis=0)
                gathered = jnp.dot(
                    tables[course], produced.astype(BF16), preferred_element_type=F32
                )
                new[:, columns] = (
                    state[:, columns].astype(F32) + gathered * scales[course]
                ).astype(BF16)


def finish(states, returned, routes, gates, experts, capacity, moment):
    tokens, width = states[0].shape
    rows, part = returned.shape[-2:]
    shape = (experts, HALVES, CORES, rows, part)
    vmem = pl.BlockSpec(memory_space=pltpu.VMEM)
    return pl.pallas_call(
        functools.partial(finish_body, capacity, moment),
        out_shape=[jax.ShapeDtypeStruct((tokens, width), BF16)] * COURSES,
        in_specs=[vmem, vmem, pl.BlockSpec(memory_space=pl.ANY), vmem, vmem],
        out_specs=[vmem] * COURSES,
        scratch_shapes=[pltpu.VMEM(shape, BF16), pltpu.SemaphoreType.DMA((2 * CORES,))],
        compiler_params=params(SMALL),
    )(*states, returned.reshape(shape), routes, gates)


def per_device(
    forward_batch, reverse_batch, norm_gain, routes, gate_values, up_weight, down_weight
):
    devices = lax.axis_size("expert")
    experts = devices // SPLIT
    states = [forward_batch[0], reverse_batch[0]]
    tokens, width = states[0].shape
    capacity = tokens // experts
    part = width // CORES
    block = (devices, COURSES * capacity, part)

    core = lax.axis_index("expert") % CORES
    up_own, down_own = up_weight[0, 0], down_weight[0, 0]
    up_got = across_cores(lax.dynamic_slice_in_dim(up_own, (1 - core) * part, part, 0))
    down_got = across_cores(lax.dynamic_slice_in_dim(down_own, (1 - core) * part, part, 1))
    up_kept = lax.dynamic_slice_in_dim(up_own, core * part, part, 0)
    down_kept = lax.dynamic_slice_in_dim(down_own, core * part, part, 1)

    lines = (COURSES, STEPS, 1, tokens)
    routes, gates = routes.reshape(lines), gate_values.reshape(lines)
    for t in range(STEPS):
        limit = LARGE if t == 0 else SMALL
        sending = prepare(states, norm_gain, routes, experts, capacity, t, limit)
        rows = exchange(sending.reshape(block)).reshape(-1, part)
        sums = up(rows, up_kept, up_got, t == 0)
        partial = down(sums, across_cores(sums), down_kept, down_got)
        returned = exchange(partial.reshape(block))
        states = finish(states, returned, routes, gates, experts, capacity, t)
        if t + 1 < STEPS:
            states = [passed_along(states[c], "section", 1 - 2 * c) for c in range(COURSES)]
    return (states[0][None], states[1][None])


def solution(mesh):
    return jax.shard_map(
        per_device,
        mesh=mesh,
        in_specs=(
            P("section", "expert", None),
            P("section", "expert", None),
            P("section", None),
            P("section", None, None, "expert", None),
            P("section", None, None, "expert", None),
            P("section", "expert", None, None),
            P("section", "expert", None, None),
        ),
        out_specs=(P("section", "expert", None), P("section", "expert", None)),
        check_vma=False,
    )
```

```python
import functools

import jax
import jax.numpy as jnp
from jax import lax
from jax.experimental import pallas as pl
from jax.experimental.pallas import tpu as pltpu
from jax.sharding import PartitionSpec as P

SPLIT = 4
STEPS = 2
CORES = 2
HALVES = SPLIT // CORES
COURSES = 2
TILE = 512
SMALL = 20 * 1024 * 1024
LARGE = 56 * 1024 * 1024

epsilon = 1e-06

F32 = jnp.float32
BF16 = jnp.bfloat16


def passed_along(array, axis, by):
    size = lax.axis_size(axis)
    return lax.ppermute(array, axis, [(i, (i + by) % size) for i in range(size)])


def across_cores(array):
    size = lax.axis_size("expert")
    return lax.ppermute(array, "expert", [(i, i ^ 1) for i in range(size)])


def exchange(blocks):
    return lax.all_to_all(blocks, "expert", split_axis=0, concat_axis=0, tiled=True)


def params(limit):
    return pltpu.CompilerParams(vmem_limit_bytes=limit)


def tiles(width):
    step = TILE if width % TILE == 0 else width
    return [(start, start + step) for start in range(0, width, step)]


def iota(shape, axis):
    return lax.broadcasted_iota(jnp.int32, shape, axis)


def slots_by_tokens(route, experts, capacity):
    tokens = route.shape[1]
    chosen = (iota((experts, tokens), 0) == route).astype(F32)
    earlier = (iota((tokens, tokens), 0) < iota((tokens, tokens), 1)).astype(BF16)
    before = jnp.dot(chosen.astype(BF16), earlier, preferred_element_type=F32)
    position = jnp.sum(chosen * before, axis=0, keepdims=True).astype(jnp.int32)
    return (iota((experts * capacity, tokens), 0) == route * capacity + position).astype(BF16)


def column(line):
    size = line.shape[1]
    same = iota((size, size), 0) == iota((size, size), 1)
    return jnp.sum(jnp.where(same, line, jnp.zeros_like(line)), axis=1, keepdims=True)


def tokens_by_slots(route, experts, capacity):
    tokens = route.shape[0]
    chosen = (iota((tokens, experts), 1) == route).astype(F32)
    earlier = (iota((tokens, tokens), 1) < iota((tokens, tokens), 0)).astype(BF16)
    before = jnp.dot(earlier, chosen.astype(BF16), preferred_element_type=F32)
    position = jnp.sum(chosen * before, axis=1, keepdims=True).astype(jnp.int32)
    return (iota((tokens, experts * capacity), 1) == route * capacity + position).astype(BF16)


def prepare_body(experts, capacity, moment, first, second, gain, routes, out, slotted, sems):
    width = first.shape[1]
    part = width // CORES
    states = (first, second)
    scales, tables = [], []
    for course, state in enumerate(states):
        total = jnp.zeros((state.shape[0], 1), F32)
        for low, high in tiles(width):
            piece = state[:, low:high].astype(F32)
            total = total + jnp.sum(piece * piece, axis=1, keepdims=True)
        scales.append(lax.rsqrt(total / width + epsilon))
        tables.append(slots_by_tokens(routes[course, moment], experts, capacity))
    copies = []
    for core in range(CORES):
        for low, high in tiles(part):
            columns = slice(core * part + low, core * part + high)
            rows = []
            for state, scale, table in zip(states, scales, tables):
                normed = (state[:, columns].astype(F32) * scale * gain[:, columns]).astype(BF16)
                rows.append(jnp.dot(table, normed, preferred_element_type=F32))
            for e in range(experts):
                span = slice(e * capacity, (e + 1) * capacity)
                block = jnp.concatenate([r[span] for r in rows], axis=0).astype(BF16)
                slotted[core, e, :, low:high] = block
        for half in range(HALVES):
            copy = pltpu.make_async_copy(
                slotted.at[core], out.at[:, half, core], sems.at[core, half]
            )
            copy.start()
            copies.append(copy)
    for copy in copies:
        copy.wait()


def prepare(states, gain, routes, experts, capacity, moment, limit):
    part = states[0].shape[1] // CORES
    rows = COURSES * capacity
    return pl.pallas_call(
        functools.partial(prepare_body, experts, capacity, moment),
        out_shape=jax.ShapeDtypeStruct((experts, HALVES, CORES, rows, part), BF16),
        in_specs=[pl.BlockSpec(memory_space=pltpu.VMEM)] * 4,
        out_specs=pl.BlockSpec(memory_space=pl.ANY),
        scratch_shapes=[
            pltpu.VMEM((CORES, experts, rows, part), BF16),
            pltpu.SemaphoreType.DMA((CORES, HALVES)),
        ],
        compiler_params=params(limit),
    )(*states, gain, routes)


def started(pairs, sems):
    copies = [pltpu.make_async_copy(*pair, sems.at[i]) for i, pair in enumerate(pairs)]
    for copy in copies:
        copy.start()
    return copies


def hold_body(*refs):
    half = (len(refs) - 1) // 2
    for copy in started(list(zip(refs[:half], refs[half:-1])), refs[-1]):
        copy.wait()


def hold(*arrays):
    return pl.pallas_call(
        hold_body,
        out_shape=[pltpu.VMEM(x.shape, x.dtype) for x in arrays],
        in_specs=[pl.BlockSpec(memory_space=pl.ANY)] * len(arrays),
        out_specs=[pl.BlockSpec(memory_space=pltpu.VMEM)] * len(arrays),
        scratch_shapes=[pltpu.SemaphoreType.DMA((len(arrays),))],
        compiler_params=params(SMALL),
    )(*arrays)


def streamed_up_body(rows, kept, got, out, rows_held, kept_held, got_held, sems):
    hidden = kept.shape[1]
    bounds = tiles(rows.shape[1])
    pairs = []
    for low, high in bounds:
        span = slice(low, high)
        pairs.append((kept.at[span], kept_held.at[span]))
        pairs.append((got.at[span], got_held.at[span]))
        pairs.append((rows.at[:, span], rows_held.at[:, span]))
    copies = started(pairs, sems)
    for i, (low, high) in enumerate(bounds):
        for copy in copies[3 * i : 3 * i + 3]:
            copy.wait()
        piece = rows_held[:, low:high]
        mine = jnp.dot(piece, kept_held[low:high], preferred_element_type=F32)
        other = jnp.dot(piece, got_held[low:high], preferred_element_type=F32)
        if i == 0:
            out[:, :hidden] = mine
            out[:, hidden:] = other
        else:
            out[:, :hidden] += mine
            out[:, hidden:] += other


def up_body(rows, kept, got, out):
    hidden = kept.shape[1]
    out[:, :hidden] = jnp.dot(rows[...], kept[...], preferred_element_type=F32)
    out[:, hidden:] = jnp.dot(rows[...], got[...], preferred_element_type=F32)


def up(rows, kept, got, streamed):
    count, part = rows.shape
    scratch = [
        pltpu.VMEM(rows.shape, BF16),
        pltpu.VMEM(kept.shape, BF16),
        pltpu.VMEM(got.shape, BF16),
        pltpu.SemaphoreType.DMA((3 * len(tiles(part)),)),
    ]
    return pl.pallas_call(
        streamed_up_body if streamed else up_body,
        out_shape=pltpu.VMEM((count, CORES * kept.shape[1]), F32),
        in_specs=[pl.BlockSpec(memory_space=pl.ANY if streamed else pltpu.VMEM)] * 3,
        out_specs=pl.BlockSpec(memory_space=pltpu.VMEM),
        scratch_shapes=scratch if streamed else [],
        compiler_params=params(LARGE if streamed else SMALL),
    )(rows, kept, got)


def down_body(mine, theirs, kept, got, out):
    hidden = kept.shape[0]
    first = jax.nn.silu(mine[:, :hidden] + theirs[:, hidden:]).astype(BF16)
    second = jax.nn.silu(mine[:, hidden:] + theirs[:, :hidden]).astype(BF16)
    for low, high in tiles(kept.shape[1]):
        total = jnp.dot(first, kept[:, low:high], preferred_element_type=F32)
        total = total + jnp.dot(second, got[:, low:high], preferred_element_type=F32)
        out[:, low:high] = total.astype(out.dtype)


def down(mine, theirs, kept, got):
    return pl.pallas_call(
        down_body,
        out_shape=jax.ShapeDtypeStruct((mine.shape[0], kept.shape[1]), BF16),
        in_specs=[pl.BlockSpec(memory_space=pltpu.VMEM)] * 4,
        out_specs=pl.BlockSpec(memory_space=pltpu.VMEM),
        compiler_params=params(SMALL),
    )(mine, theirs, kept, got)


def finish_body(
    capacity, moment, first, second, returned, routes, gates, new_first, new_second, held, sems
):
    experts = returned.shape[0]
    part = returned.shape[-1]
    step = part // 2
    spans = [(core, low) for core in range(CORES) for low in (0, step)]
    copies = started(
        [
            (
                returned.at[:, :, core, :, low : low + step],
                held.at[:, :, core, :, low : low + step],
            )
            for core, low in spans
        ],
        sems,
    )
    chosen = [column(routes[course, moment]) for course in range(COURSES)]
    tables = [tokens_by_slots(route, experts, capacity) for route in chosen]
    scales = [column(gates[course, moment]) for course in range(COURSES)]
    for copy, (core, start) in zip(copies, spans):
        copy.wait()
        for low in range(start, start + step, TILE // 2):
            high = low + TILE // 2
            summed = [
                held[e, 0, core, :, low:high].astype(F32)
                + held[e, 1, core, :, low:high].astype(F32)
                for e in range(experts)
            ]
            columns = slice(core * part + low, core * part + high)
            for course, (state, new) in enumerate(((first, new_first), (second, new_second))):
                span = slice(course * capacity, (course + 1) * capacity)
                produced = jnp.concatenate([block[span] for block in summed], axis=0)
                gathered = jnp.dot(
                    tables[course], produced.astype(BF16), preferred_element_type=F32
                )
                new[:, columns] = (
                    state[:, columns].astype(F32) + gathered * scales[course]
                ).astype(BF16)


def finish(states, returned, routes, gates, experts, capacity, moment):
    tokens, width = states[0].shape
    rows, part = returned.shape[-2:]
    shape = (experts, HALVES, CORES, rows, part)
    vmem = pl.BlockSpec(memory_space=pltpu.VMEM)
    return pl.pallas_call(
        functools.partial(finish_body, capacity, moment),
        out_shape=[jax.ShapeDtypeStruct((tokens, width), BF16)] * COURSES,
        in_specs=[vmem, vmem, pl.BlockSpec(memory_space=pl.ANY), vmem, vmem],
        out_specs=[vmem] * COURSES,
        scratch_shapes=[pltpu.VMEM(shape, BF16), pltpu.SemaphoreType.DMA((2 * CORES,))],
        compiler_params=params(SMALL),
    )(*states, returned.reshape(shape), routes, gates)


def per_device(
    forward_batch, reverse_batch, norm_gain, routes, gate_values, up_weight, down_weight
):
    devices = lax.axis_size("expert")
    experts = devices // SPLIT
    states = [forward_batch[0], reverse_batch[0]]
    tokens, width = states[0].shape
    capacity = tokens // experts
    part = width // CORES
    block = (devices, COURSES * capacity, part)

    core = lax.axis_index("expert") % CORES
    up_own, down_own = up_weight[0, 0], down_weight[0, 0]
    up_got = across_cores(lax.dynamic_slice_in_dim(up_own, (1 - core) * part, part, 0))
    down_got = across_cores(lax.dynamic_slice_in_dim(down_own, (1 - core) * part, part, 1))
    up_kept = lax.dynamic_slice_in_dim(up_own, core * part, part, 0)
    down_kept = lax.dynamic_slice_in_dim(down_own, core * part, part, 1)

    near_down = hold(down_kept, down_got)
    lines = (COURSES, STEPS, 1, tokens)
    routes, gates = routes.reshape(lines), gate_values.reshape(lines)
    for t in range(STEPS):
        limit = LARGE if t == 0 else SMALL
        sending = prepare(states, norm_gain, routes, experts, capacity, t, limit)
        rows = exchange(sending.reshape(block)).reshape(-1, part)
        rows, near_down = lax.optimization_barrier((rows, near_down))
        sums = up(rows, up_kept, up_got, True) if t == 0 else up(rows, *near_up, False)
        partial = down(sums, across_cores(sums), *near_down)
        returned = exchange(partial.reshape(block))
        states = finish(states, returned, routes, gates, experts, capacity, t)
        if t + 1 < STEPS:
            up_kept, up_got, *states = lax.optimization_barrier((up_kept, up_got, *states))
            near_up = hold(up_kept, up_got)
            states = [passed_along(states[c], "section", 1 - 2 * c) for c in range(COURSES)]
            states, near_up = lax.optimization_barrier((states, near_up))
    return (states[0][None], states[1][None])


def solution(mesh):
    return jax.shard_map(
        per_device,
        mesh=mesh,
        in_specs=(
            P("section", "expert", None),
            P("section", "expert", None),
            P("section", None),
            P("section", None, None, "expert", None),
            P("section", None, None, "expert", None),
            P("section", "expert", None, None),
            P("section", "expert", None, None),
        ),
        out_specs=(P("section", "expert", None), P("section", "expert", None)),
        check_vma=False,
    )
```

```python
import functools

import jax
import jax.numpy as jnp
from jax import lax
from jax.experimental import pallas as pl
from jax.experimental.pallas import tpu as pltpu
from jax.sharding import PartitionSpec as P

SPLIT = 4
STEPS = 2
CORES = 2
HALVES = SPLIT // CORES
COURSES = 2
TILE = 512
SMALL = 20 * 1024 * 1024
LARGE = 56 * 1024 * 1024

epsilon = 1e-06

F32 = jnp.float32
BF16 = jnp.bfloat16


def passed_along(array, axis, by):
    size = lax.axis_size(axis)
    return lax.ppermute(array, axis, [(i, (i + by) % size) for i in range(size)])


def across_cores(array):
    size = lax.axis_size("expert")
    return lax.ppermute(array, "expert", [(i, i ^ 1) for i in range(size)])


def exchange(blocks):
    return lax.all_to_all(blocks, "expert", split_axis=0, concat_axis=0, tiled=True)


def params(limit):
    return pltpu.CompilerParams(vmem_limit_bytes=limit)


def tiles(width):
    step = TILE if width % TILE == 0 else width
    return [(start, start + step) for start in range(0, width, step)]


def iota(shape, axis):
    return lax.broadcasted_iota(jnp.int32, shape, axis)


def slots_by_tokens(route, experts, capacity):
    tokens = route.shape[1]
    chosen = (iota((experts, tokens), 0) == route).astype(F32)
    earlier = (iota((tokens, tokens), 0) < iota((tokens, tokens), 1)).astype(BF16)
    before = jnp.dot(chosen.astype(BF16), earlier, preferred_element_type=F32)
    position = jnp.sum(chosen * before, axis=0, keepdims=True).astype(jnp.int32)
    return (iota((experts * capacity, tokens), 0) == route * capacity + position).astype(BF16)


def column(line):
    size = line.shape[1]
    same = iota((size, size), 0) == iota((size, size), 1)
    return jnp.sum(jnp.where(same, line, jnp.zeros_like(line)), axis=1, keepdims=True)


def tokens_by_slots(route, experts, capacity):
    tokens = route.shape[0]
    chosen = (iota((tokens, experts), 1) == route).astype(F32)
    earlier = (iota((tokens, tokens), 1) < iota((tokens, tokens), 0)).astype(BF16)
    before = jnp.dot(earlier, chosen.astype(BF16), preferred_element_type=F32)
    position = jnp.sum(chosen * before, axis=1, keepdims=True).astype(jnp.int32)
    return (iota((tokens, experts * capacity), 1) == route * capacity + position).astype(BF16)


def prepare_body(experts, capacity, moment, first, second, gain, routes, out, slotted, sems):
    width = first.shape[1]
    part = width // CORES
    states = (first, second)
    scales, tables = [], []
    for course, state in enumerate(states):
        total = jnp.zeros((state.shape[0], 1), F32)
        for low, high in tiles(width):
            piece = state[:, low:high].astype(F32)
            total = total + jnp.sum(piece * piece, axis=1, keepdims=True)
        scales.append(lax.rsqrt(total / width + epsilon))
        tables.append(slots_by_tokens(routes[course, moment], experts, capacity))
    copies = []
    for core in range(CORES):
        for low, high in tiles(part):
            columns = slice(core * part + low, core * part + high)
            rows = []
            for state, scale, table in zip(states, scales, tables):
                normed = (state[:, columns].astype(F32) * scale * gain[:, columns]).astype(BF16)
                rows.append(jnp.dot(table, normed, preferred_element_type=F32))
            for e in range(experts):
                span = slice(e * capacity, (e + 1) * capacity)
                block = jnp.concatenate([r[span] for r in rows], axis=0).astype(BF16)
                slotted[core, e, :, low:high] = block
        for half in range(HALVES):
            copy = pltpu.make_async_copy(
                slotted.at[core], out.at[:, half, core], sems.at[core, half]
            )
            copy.start()
            copies.append(copy)
    for copy in copies:
        copy.wait()


def prepare(states, gain, routes, experts, capacity, moment, limit):
    part = states[0].shape[1] // CORES
    rows = COURSES * capacity
    return pl.pallas_call(
        functools.partial(prepare_body, experts, capacity, moment),
        out_shape=jax.ShapeDtypeStruct((experts, HALVES, CORES, rows, part), BF16),
        in_specs=[pl.BlockSpec(memory_space=pltpu.VMEM)] * 4,
        out_specs=pl.BlockSpec(memory_space=pl.ANY),
        scratch_shapes=[
            pltpu.VMEM((CORES, experts, rows, part), BF16),
            pltpu.SemaphoreType.DMA((CORES, HALVES)),
        ],
        compiler_params=params(limit),
    )(*states, gain, routes)


def started(pairs, sems):
    copies = [pltpu.make_async_copy(*pair, sems.at[i]) for i, pair in enumerate(pairs)]
    for copy in copies:
        copy.start()
    return copies


def hold_body(*refs):
    half = (len(refs) - 1) // 2
    for copy in started(list(zip(refs[:half], refs[half:-1])), refs[-1]):
        copy.wait()


def hold(*arrays):
    return pl.pallas_call(
        hold_body,
        out_shape=[pltpu.VMEM(x.shape, x.dtype) for x in arrays],
        in_specs=[pl.BlockSpec(memory_space=pl.ANY)] * len(arrays),
        out_specs=[pl.BlockSpec(memory_space=pltpu.VMEM)] * len(arrays),
        scratch_shapes=[pltpu.SemaphoreType.DMA((len(arrays),))],
        compiler_params=params(SMALL),
    )(*arrays)


def streamed_up_body(rows, kept, got, out, rows_held, kept_held, got_held, sems):
    hidden = kept.shape[1]
    bounds = tiles(rows.shape[1])
    pairs = []
    for low, high in bounds:
        span = slice(low, high)
        pairs.append((kept.at[span], kept_held.at[span]))
        pairs.append((got.at[span], got_held.at[span]))
        pairs.append((rows.at[:, span], rows_held.at[:, span]))
    copies = started(pairs, sems)
    for i, (low, high) in enumerate(bounds):
        for copy in copies[3 * i : 3 * i + 3]:
            copy.wait()
        piece = rows_held[:, low:high]
        mine = jnp.dot(piece, kept_held[low:high], preferred_element_type=F32)
        other = jnp.dot(piece, got_held[low:high], preferred_element_type=F32)
        if i == 0:
            out[:, :hidden] = mine
            out[:, hidden:] = other
        else:
            out[:, :hidden] += mine
            out[:, hidden:] += other


def up_body(low, rows, kept, got, out):
    hidden = kept.shape[1]
    piece = rows[low : low + out.shape[0]]
    out[:, :hidden] = jnp.dot(piece, kept[...], preferred_element_type=F32)
    out[:, hidden:] = jnp.dot(piece, got[...], preferred_element_type=F32)


def streamed_up(rows, kept, got):
    count, part = rows.shape
    return pl.pallas_call(
        streamed_up_body,
        out_shape=pltpu.VMEM((count, CORES * kept.shape[1]), F32),
        in_specs=[pl.BlockSpec(memory_space=pl.ANY)] * 3,
        out_specs=pl.BlockSpec(memory_space=pltpu.VMEM),
        scratch_shapes=[
            pltpu.VMEM(rows.shape, BF16),
            pltpu.VMEM(kept.shape, BF16),
            pltpu.VMEM(got.shape, BF16),
            pltpu.SemaphoreType.DMA((3 * len(tiles(part)),)),
        ],
        compiler_params=params(LARGE),
    )(rows, kept, got)


def up(rows, kept, got, low, count):
    return pl.pallas_call(
        functools.partial(up_body, low),
        out_shape=pltpu.VMEM((count, CORES * kept.shape[1]), F32),
        in_specs=[pl.BlockSpec(memory_space=pltpu.VMEM)] * 3,
        out_specs=pl.BlockSpec(memory_space=pltpu.VMEM),
        compiler_params=params(SMALL),
    )(rows, kept, got)


def down_body(*refs):
    sums, (kept, got, out) = refs[:-3], refs[-3:]
    hidden = kept.shape[0]
    active = []
    for mine, theirs in zip(sums[0::2], sums[1::2]):
        first = jax.nn.silu(mine[:, :hidden] + theirs[:, hidden:]).astype(BF16)
        second = jax.nn.silu(mine[:, hidden:] + theirs[:, :hidden]).astype(BF16)
        active.append((first, second))
    for low, high in tiles(kept.shape[1]):
        for i, (first, second) in enumerate(active):
            rows = slice(i * first.shape[0], (i + 1) * first.shape[0])
            total = jnp.dot(first, kept[:, low:high], preferred_element_type=F32)
            total = total + jnp.dot(second, got[:, low:high], preferred_element_type=F32)
            out[rows, low:high] = total.astype(out.dtype)


def down(sums, kept, got):
    count = sum(x.shape[0] for x in sums[0::2])
    return pl.pallas_call(
        down_body,
        out_shape=jax.ShapeDtypeStruct((count, kept.shape[1]), BF16),
        in_specs=[pl.BlockSpec(memory_space=pltpu.VMEM)] * (len(sums) + 2),
        out_specs=pl.BlockSpec(memory_space=pltpu.VMEM),
        compiler_params=params(SMALL),
    )(*sums, kept, got)


def finish_body(capacity, moment, first, second, returned, routes, gates, *refs):
    outs, rest = refs[:COURSES], refs[COURSES:]
    news = rest[:COURSES] if rest else outs
    experts = returned.shape[0]
    part = returned.shape[-1]
    chosen = [column(routes[course, moment]) for course in range(COURSES)]
    tables = [tokens_by_slots(route, experts, capacity) for route in chosen]
    scales = [column(gates[course, moment]) for course in range(COURSES)]
    leaving = []
    for core in range(CORES):
        for low in range(0, part, TILE // 2):
            high = low + TILE // 2
            summed = [
                returned[e, 0, core, :, low:high].astype(F32)
                + returned[e, 1, core, :, low:high].astype(F32)
                for e in range(experts)
            ]
            columns = slice(core * part + low, core * part + high)
            for course, (state, new) in enumerate(((first, news[0]), (second, news[1]))):
                span = slice(course * capacity, (course + 1) * capacity)
                produced = jnp.concatenate([block[span] for block in summed], axis=0)
                gathered = jnp.dot(
                    tables[course], produced.astype(BF16), preferred_element_type=F32
                )
                new[:, columns] = (
                    state[:, columns].astype(F32) + gathered * scales[course]
                ).astype(BF16)
        if rest:
            span = slice(core * part, (core + 1) * part)
            for course in range(COURSES):
                copy = pltpu.make_async_copy(
                    news[course].at[:, span],
                    outs[course].at[:, span],
                    rest[COURSES].at[core, course],
                )
                copy.start()
                leaving.append(copy)
    for copy in leaving:
        copy.wait()


def finish(states, returned, routes, gates, experts, capacity, moment, last):
    tokens, width = states[0].shape
    rows, part = returned.shape[-2:]
    shape = (experts, HALVES, CORES, rows, part)
    vmem = pl.BlockSpec(memory_space=pltpu.VMEM)
    scratch = [pltpu.VMEM((tokens, width), BF16)] * COURSES
    scratch.append(pltpu.SemaphoreType.DMA((CORES, COURSES)))
    return pl.pallas_call(
        functools.partial(finish_body, capacity, moment),
        out_shape=[jax.ShapeDtypeStruct((tokens, width), BF16)] * COURSES,
        in_specs=[vmem] * 5,
        out_specs=[pl.BlockSpec(memory_space=pl.ANY) if last else vmem] * COURSES,
        scratch_shapes=scratch if last else [],
        compiler_params=params(SMALL),
    )(*states, returned.reshape(shape), routes, gates)


def per_device(
    forward_batch, reverse_batch, norm_gain, routes, gate_values, up_weight, down_weight
):
    devices = lax.axis_size("expert")
    experts = devices // SPLIT
    states = [forward_batch[0], reverse_batch[0]]
    tokens, width = states[0].shape
    capacity = tokens // experts
    part = width // CORES
    block = (devices, COURSES * capacity, part)

    core = lax.axis_index("expert") % CORES
    up_own, down_own = up_weight[0, 0], down_weight[0, 0]
    up_got = across_cores(lax.dynamic_slice_in_dim(up_own, (1 - core) * part, part, 0))
    down_got = across_cores(lax.dynamic_slice_in_dim(down_own, (1 - core) * part, part, 1))
    up_kept = lax.dynamic_slice_in_dim(up_own, core * part, part, 0)
    down_kept = lax.dynamic_slice_in_dim(down_own, core * part, part, 1)

    near_down = hold(down_kept, down_got)
    lines = (COURSES, STEPS, 1, tokens)
    routes, gates = routes.reshape(lines), gate_values.reshape(lines)
    for t in range(STEPS):
        limit = LARGE if t == 0 else SMALL
        sending = prepare(states, norm_gain, routes, experts, capacity, t, limit)
        rows = exchange(sending.reshape(block)).reshape(-1, part)
        rows, near_down = lax.optimization_barrier((rows, near_down))
        if t == 0:
            sums = [streamed_up(rows, up_kept, up_got)]
        else:
            half = rows.shape[0] // 2
            sums = [up(rows, *near_up, low, half) for low in (0, half)]
        partial = down([x for mine in sums for x in (mine, across_cores(mine))], *near_down)
        returned = exchange(partial.reshape(block))
        last = t + 1 == STEPS
        states = finish(states, returned, routes, gates, experts, capacity, t, last)
        if not last:
            up_kept, up_got, *states = lax.optimization_barrier((up_kept, up_got, *states))
            near_up = hold(up_kept, up_got)
            states = [passed_along(states[c], "section", 1 - 2 * c) for c in range(COURSES)]
            states, near_up = lax.optimization_barrier((states, near_up))
    return (states[0][None], states[1][None])


def solution(mesh):
    return jax.shard_map(
        per_device,
        mesh=mesh,
        in_specs=(
            P("section", "expert", None),
            P("section", "expert", None),
            P("section", None),
            P("section", None, None, "expert", None),
            P("section", None, None, "expert", None),
            P("section", "expert", None, None),
            P("section", "expert", None, None),
        ),
        out_specs=(P("section", "expert", None), P("section", "expert", None)),
        check_vma=False,
    )
```

```python
import functools

import jax
import jax.numpy as jnp
from jax import lax
from jax.experimental import pallas as pl
from jax.experimental.pallas import tpu as pltpu
from jax.sharding import PartitionSpec as P

SPLIT = 4
STEPS = 2
CORES = 2
HALVES = SPLIT // CORES
COURSES = 2
TILE = 512
SMALL = 20 * 1024 * 1024
LARGE = 56 * 1024 * 1024

epsilon = 1e-06

F32 = jnp.float32
BF16 = jnp.bfloat16


def passed_along(array, axis, by):
    size = lax.axis_size(axis)
    return lax.ppermute(array, axis, [(i, (i + by) % size) for i in range(size)])


def across_cores(array):
    size = lax.axis_size("expert")
    return lax.ppermute(array, "expert", [(i, i ^ 1) for i in range(size)])


def exchange(blocks):
    return lax.all_to_all(blocks, "expert", split_axis=0, concat_axis=0, tiled=True)


def params(limit):
    return pltpu.CompilerParams(vmem_limit_bytes=limit)


def tiles(width):
    step = TILE if width % TILE == 0 else width
    return [(start, start + step) for start in range(0, width, step)]


def iota(shape, axis):
    return lax.broadcasted_iota(jnp.int32, shape, axis)


def slots_by_tokens(route, experts, capacity):
    tokens = route.shape[1]
    chosen = (iota((experts, tokens), 0) == route).astype(F32)
    earlier = (iota((tokens, tokens), 0) < iota((tokens, tokens), 1)).astype(BF16)
    before = jnp.dot(chosen.astype(BF16), earlier, preferred_element_type=F32)
    position = jnp.sum(chosen * before, axis=0, keepdims=True).astype(jnp.int32)
    return (iota((experts * capacity, tokens), 0) == route * capacity + position).astype(BF16)


def column(line):
    size = line.shape[1]
    same = iota((size, size), 0) == iota((size, size), 1)
    return jnp.sum(jnp.where(same, line, jnp.zeros_like(line)), axis=1, keepdims=True)


def tokens_by_slots(route, experts, capacity):
    tokens = route.shape[0]
    chosen = (iota((tokens, experts), 1) == route).astype(F32)
    earlier = (iota((tokens, tokens), 1) < iota((tokens, tokens), 0)).astype(BF16)
    before = jnp.dot(earlier, chosen.astype(BF16), preferred_element_type=F32)
    position = jnp.sum(chosen * before, axis=1, keepdims=True).astype(jnp.int32)
    return (iota((tokens, experts * capacity), 1) == route * capacity + position).astype(BF16)


def prepare_body(experts, capacity, moment, first, second, gain, routes, out, slotted, sems):
    width = first.shape[1]
    part = width // CORES
    states = (first, second)
    scales, tables = [], []
    for course, state in enumerate(states):
        total = jnp.zeros((state.shape[0], 1), F32)
        for low, high in tiles(width):
            piece = state[:, low:high].astype(F32)
            total = total + jnp.sum(piece * piece, axis=1, keepdims=True)
        scales.append(lax.rsqrt(total / width + epsilon))
        tables.append(slots_by_tokens(routes[course, moment], experts, capacity))
    copies = []
    for core in range(CORES):
        for low, high in tiles(part):
            columns = slice(core * part + low, core * part + high)
            rows = []
            for state, scale, table in zip(states, scales, tables):
                normed = (state[:, columns].astype(F32) * scale * gain[:, columns]).astype(BF16)
                rows.append(jnp.dot(table, normed, preferred_element_type=F32))
            for e in range(experts):
                span = slice(e * capacity, (e + 1) * capacity)
                block = jnp.concatenate([r[span] for r in rows], axis=0).astype(BF16)
                slotted[core, e, :, low:high] = block
        for half in range(HALVES):
            copy = pltpu.make_async_copy(
                slotted.at[core], out.at[:, half, core], sems.at[core, half]
            )
            copy.start()
            copies.append(copy)
    for copy in copies:
        copy.wait()


def prepare(states, gain, routes, experts, capacity, moment, limit):
    part = states[0].shape[1] // CORES
    rows = COURSES * capacity
    return pl.pallas_call(
        functools.partial(prepare_body, experts, capacity, moment),
        out_shape=jax.ShapeDtypeStruct((experts, HALVES, CORES, rows, part), BF16),
        in_specs=[pl.BlockSpec(memory_space=pltpu.VMEM)] * 4,
        out_specs=pl.BlockSpec(memory_space=pl.ANY),
        scratch_shapes=[
            pltpu.VMEM((CORES, experts, rows, part), BF16),
            pltpu.SemaphoreType.DMA((CORES, HALVES)),
        ],
        compiler_params=params(limit),
    )(*states, gain, routes)


def started(pairs, sems):
    copies = [pltpu.make_async_copy(*pair, sems.at[i]) for i, pair in enumerate(pairs)]
    for copy in copies:
        copy.start()
    return copies


def hold_body(*refs):
    half = (len(refs) - 1) // 2
    for copy in started(list(zip(refs[:half], refs[half:-1])), refs[-1]):
        copy.wait()


def hold(*arrays):
    return pl.pallas_call(
        hold_body,
        out_shape=[pltpu.VMEM(x.shape, x.dtype) for x in arrays],
        in_specs=[pl.BlockSpec(memory_space=pl.ANY)] * len(arrays),
        out_specs=[pl.BlockSpec(memory_space=pltpu.VMEM)] * len(arrays),
        scratch_shapes=[pltpu.SemaphoreType.DMA((len(arrays),))],
        compiler_params=params(SMALL),
    )(*arrays)


def streamed_up_body(rows, kept, got, out, rows_held, kept_held, got_held, sems):
    hidden = kept.shape[1]
    bounds = tiles(rows.shape[1])
    pairs = []
    for low, high in bounds:
        span = slice(low, high)
        pairs.append((kept.at[span], kept_held.at[span]))
        pairs.append((got.at[span], got_held.at[span]))
        pairs.append((rows.at[:, span], rows_held.at[:, span]))
    copies = started(pairs, sems)
    for i, (low, high) in enumerate(bounds):
        for copy in copies[3 * i : 3 * i + 3]:
            copy.wait()
        piece = rows_held[:, low:high]
        mine = jnp.dot(piece, kept_held[low:high], preferred_element_type=F32)
        other = jnp.dot(piece, got_held[low:high], preferred_element_type=F32)
        if i == 0:
            out[:, :hidden] = mine
            out[:, hidden:] = other
        else:
            out[:, :hidden] += mine
            out[:, hidden:] += other


def up_body(rows, kept, got, out):
    hidden = kept.shape[1]
    out[:, :hidden] = jnp.dot(rows[...], kept[...], preferred_element_type=F32)
    out[:, hidden:] = jnp.dot(rows[...], got[...], preferred_element_type=F32)


def streamed_up(rows, kept, got):
    count, part = rows.shape
    return pl.pallas_call(
        streamed_up_body,
        out_shape=pltpu.VMEM((count, CORES * kept.shape[1]), F32),
        in_specs=[pl.BlockSpec(memory_space=pl.ANY)] * 3,
        out_specs=pl.BlockSpec(memory_space=pltpu.VMEM),
        scratch_shapes=[
            pltpu.VMEM(rows.shape, BF16),
            pltpu.VMEM(kept.shape, BF16),
            pltpu.VMEM(got.shape, BF16),
            pltpu.SemaphoreType.DMA((3 * len(tiles(part)),)),
        ],
        compiler_params=params(LARGE),
    )(rows, kept, got)


def up(rows, kept, got):
    return pl.pallas_call(
        up_body,
        out_shape=pltpu.VMEM((rows.shape[0], CORES * kept.shape[1]), F32),
        in_specs=[pl.BlockSpec(memory_space=pltpu.VMEM)] * 3,
        out_specs=pl.BlockSpec(memory_space=pltpu.VMEM),
        compiler_params=params(SMALL),
    )(rows, kept, got)


def down_body(*refs):
    sums, (kept, got, out) = refs[:-3], refs[-3:]
    hidden = kept.shape[0]
    active = []
    for mine, theirs in zip(sums[0::2], sums[1::2]):
        first = jax.nn.silu(mine[:, :hidden] + theirs[:, hidden:]).astype(BF16)
        second = jax.nn.silu(mine[:, hidden:] + theirs[:, :hidden]).astype(BF16)
        active.append((first, second))
    for low, high in tiles(kept.shape[1]):
        for i, (first, second) in enumerate(active):
            rows = slice(i * first.shape[0], (i + 1) * first.shape[0])
            total = jnp.dot(first, kept[:, low:high], preferred_element_type=F32)
            total = total + jnp.dot(second, got[:, low:high], preferred_element_type=F32)
            out[rows, low:high] = total.astype(out.dtype)


def down(sums, kept, got):
    count = sum(x.shape[0] for x in sums[0::2])
    return pl.pallas_call(
        down_body,
        out_shape=jax.ShapeDtypeStruct((count, kept.shape[1]), BF16),
        in_specs=[pl.BlockSpec(memory_space=pltpu.VMEM)] * (len(sums) + 2),
        out_specs=pl.BlockSpec(memory_space=pltpu.VMEM),
        compiler_params=params(SMALL),
    )(*sums, kept, got)


def finish_body(capacity, moment, first, second, returned, routes, gates, *refs):
    outs, rest = refs[:COURSES], refs[COURSES:]
    news = rest[:COURSES] if rest else outs
    experts = returned.shape[0]
    part = returned.shape[-1]
    chosen = [column(routes[course, moment]) for course in range(COURSES)]
    tables = [tokens_by_slots(route, experts, capacity) for route in chosen]
    scales = [column(gates[course, moment]) for course in range(COURSES)]
    leaving = []
    for core in range(CORES):
        for low in range(0, part, TILE // 2):
            high = low + TILE // 2
            summed = [
                returned[e, 0, core, :, low:high].astype(F32)
                + returned[e, 1, core, :, low:high].astype(F32)
                for e in range(experts)
            ]
            columns = slice(core * part + low, core * part + high)
            for course, (state, new) in enumerate(((first, news[0]), (second, news[1]))):
                span = slice(course * capacity, (course + 1) * capacity)
                produced = jnp.concatenate([block[span] for block in summed], axis=0)
                gathered = jnp.dot(
                    tables[course], produced.astype(BF16), preferred_element_type=F32
                )
                new[:, columns] = (
                    state[:, columns].astype(F32) + gathered * scales[course]
                ).astype(BF16)
        if rest:
            span = slice(core * part, (core + 1) * part)
            for course in range(COURSES):
                copy = pltpu.make_async_copy(
                    news[course].at[:, span],
                    outs[course].at[:, span],
                    rest[COURSES].at[core, course],
                )
                copy.start()
                leaving.append(copy)
    for copy in leaving:
        copy.wait()


def finish(states, returned, routes, gates, experts, capacity, moment, last):
    tokens, width = states[0].shape
    rows, part = returned.shape[-2:]
    shape = (experts, HALVES, CORES, rows, part)
    vmem = pl.BlockSpec(memory_space=pltpu.VMEM)
    scratch = [pltpu.VMEM((tokens, width), BF16)] * COURSES
    scratch.append(pltpu.SemaphoreType.DMA((CORES, COURSES)))
    return pl.pallas_call(
        functools.partial(finish_body, capacity, moment),
        out_shape=[jax.ShapeDtypeStruct((tokens, width), BF16)] * COURSES,
        in_specs=[vmem] * 5,
        out_specs=[pl.BlockSpec(memory_space=pl.ANY) if last else vmem] * COURSES,
        scratch_shapes=scratch if last else [],
        compiler_params=params(SMALL),
    )(*states, returned.reshape(shape), routes, gates)


def per_device(
    forward_batch, reverse_batch, norm_gain, routes, gate_values, up_weight, down_weight
):
    devices = lax.axis_size("expert")
    experts = devices // SPLIT
    states = [forward_batch[0], reverse_batch[0]]
    tokens, width = states[0].shape
    capacity = tokens // experts
    part = width // CORES
    block = (devices, COURSES * capacity, part)

    core = lax.axis_index("expert") % CORES
    up_own, down_own = up_weight[0, 0], down_weight[0, 0]
    up_got = across_cores(lax.dynamic_slice_in_dim(up_own, (1 - core) * part, part, 0))
    down_got = across_cores(lax.dynamic_slice_in_dim(down_own, (1 - core) * part, part, 1))
    up_kept = lax.dynamic_slice_in_dim(up_own, core * part, part, 0)
    down_kept = lax.dynamic_slice_in_dim(down_own, core * part, part, 1)

    near_down = hold(down_kept, down_got)
    lines = (COURSES, STEPS, 1, tokens)
    routes, gates = routes.reshape(lines), gate_values.reshape(lines)
    for t in range(STEPS):
        limit = LARGE if t == 0 else SMALL
        sending = prepare(states, norm_gain, routes, experts, capacity, t, limit)
        rows = exchange(sending.reshape(block)).reshape(-1, part)
        rows, near_down = lax.optimization_barrier((rows, near_down))
        if t == 0:
            sums = [streamed_up(rows, up_kept, up_got)]
        else:
            sums = [up(rows, *near_up)]
        partial = down([x for mine in sums for x in (mine, across_cores(mine))], *near_down)
        returned = exchange(partial.reshape(block))
        last = t + 1 == STEPS
        states = finish(states, returned, routes, gates, experts, capacity, t, last)
        if not last:
            up_kept, up_got, *states = lax.optimization_barrier((up_kept, up_got, *states))
            near_up = hold(up_kept, up_got)
            states = [passed_along(states[c], "section", 1 - 2 * c) for c in range(COURSES)]
            states, near_up = lax.optimization_barrier((states, near_up))
    return (states[0][None], states[1][None])


def solution(mesh):
    return jax.shard_map(
        per_device,
        mesh=mesh,
        in_specs=(
            P("section", "expert", None),
            P("section", "expert", None),
            P("section", None),
            P("section", None, None, "expert", None),
            P("section", None, None, "expert", None),
            P("section", "expert", None, None),
            P("section", "expert", None, None),
        ),
        out_specs=(P("section", "expert", None), P("section", "expert", None)),
        check_vma=False,
    )
```

```python
import functools

import jax
import jax.numpy as jnp
from jax import lax
from jax.experimental import pallas as pl
from jax.experimental.pallas import tpu as pltpu
from jax.sharding import PartitionSpec as P

SPLIT = 4
STEPS = 2
CORES = 2
HALVES = SPLIT // CORES
COURSES = 2
TILE = 512
SMALL = 20 * 1024 * 1024
LARGE = 56 * 1024 * 1024

epsilon = 1e-06

F32 = jnp.float32
BF16 = jnp.bfloat16


def passed_along(array, axis, by):
    size = lax.axis_size(axis)
    return lax.ppermute(array, axis, [(i, (i + by) % size) for i in range(size)])


def across_cores(array):
    size = lax.axis_size("expert")
    return lax.ppermute(array, "expert", [(i, i ^ 1) for i in range(size)])


def exchange(blocks):
    return lax.all_to_all(blocks, "expert", split_axis=0, concat_axis=0, tiled=True)


def params(limit):
    return pltpu.CompilerParams(vmem_limit_bytes=limit)


def tiles(width):
    step = TILE if width % TILE == 0 else width
    return [(start, start + step) for start in range(0, width, step)]


def iota(shape, axis):
    return lax.broadcasted_iota(jnp.int32, shape, axis)


def slots_by_tokens(route, experts, capacity):
    tokens = route.shape[1]
    chosen = (iota((experts, tokens), 0) == route).astype(F32)
    earlier = (iota((tokens, tokens), 0) < iota((tokens, tokens), 1)).astype(BF16)
    before = jnp.dot(chosen.astype(BF16), earlier, preferred_element_type=F32)
    position = jnp.sum(chosen * before, axis=0, keepdims=True).astype(jnp.int32)
    return (iota((experts * capacity, tokens), 0) == route * capacity + position).astype(BF16)


def column(line):
    size = line.shape[1]
    same = iota((size, size), 0) == iota((size, size), 1)
    return jnp.sum(jnp.where(same, line, jnp.zeros_like(line)), axis=1, keepdims=True)


def tokens_by_slots(route, experts, capacity):
    tokens = route.shape[0]
    chosen = (iota((tokens, experts), 1) == route).astype(F32)
    earlier = (iota((tokens, tokens), 1) < iota((tokens, tokens), 0)).astype(BF16)
    before = jnp.dot(earlier, chosen.astype(BF16), preferred_element_type=F32)
    position = jnp.sum(chosen * before, axis=1, keepdims=True).astype(jnp.int32)
    return (iota((tokens, experts * capacity), 1) == route * capacity + position).astype(BF16)


def prepare_body(experts, capacity, moment, first, second, gain, routes, out, slotted, sems):
    width = first.shape[1]
    part = width // CORES
    states = (first, second)
    scales, tables = [], []
    for course, state in enumerate(states):
        total = jnp.zeros((state.shape[0], 1), F32)
        for low, high in tiles(width):
            piece = state[:, low:high].astype(F32)
            total = total + jnp.sum(piece * piece, axis=1, keepdims=True)
        scales.append(lax.rsqrt(total / width + epsilon))
        tables.append(slots_by_tokens(routes[course, moment], experts, capacity))
    copies = []
    for core in range(CORES):
        for low, high in tiles(part):
            columns = slice(core * part + low, core * part + high)
            rows = []
            for state, scale, table in zip(states, scales, tables):
                normed = (state[:, columns].astype(F32) * scale * gain[:, columns]).astype(BF16)
                rows.append(jnp.dot(table, normed, preferred_element_type=F32))
            for e in range(experts):
                span = slice(e * capacity, (e + 1) * capacity)
                block = jnp.concatenate([r[span] for r in rows], axis=0).astype(BF16)
                slotted[core, e, :, low:high] = block
        for half in range(HALVES):
            copy = pltpu.make_async_copy(
                slotted.at[core], out.at[:, half, core], sems.at[core, half]
            )
            copy.start()
            copies.append(copy)
    for copy in copies:
        copy.wait()


def prepare(states, gain, routes, experts, capacity, moment, limit):
    part = states[0].shape[1] // CORES
    rows = COURSES * capacity
    return pl.pallas_call(
        functools.partial(prepare_body, experts, capacity, moment),
        out_shape=jax.ShapeDtypeStruct((experts, HALVES, CORES, rows, part), BF16),
        in_specs=[pl.BlockSpec(memory_space=pltpu.VMEM)] * 4,
        out_specs=pl.BlockSpec(memory_space=pl.ANY),
        scratch_shapes=[
            pltpu.VMEM((CORES, experts, rows, part), BF16),
            pltpu.SemaphoreType.DMA((CORES, HALVES)),
        ],
        compiler_params=params(limit),
    )(*states, gain, routes)


def started(pairs, sems):
    copies = [pltpu.make_async_copy(*pair, sems.at[i]) for i, pair in enumerate(pairs)]
    for copy in copies:
        copy.start()
    return copies


def hold_body(*refs):
    half = (len(refs) - 1) // 2
    for copy in started(list(zip(refs[:half], refs[half:-1])), refs[-1]):
        copy.wait()


def hold(*arrays):
    return pl.pallas_call(
        hold_body,
        out_shape=[pltpu.VMEM(x.shape, x.dtype) for x in arrays],
        in_specs=[pl.BlockSpec(memory_space=pl.ANY)] * len(arrays),
        out_specs=[pl.BlockSpec(memory_space=pltpu.VMEM)] * len(arrays),
        scratch_shapes=[pltpu.SemaphoreType.DMA((len(arrays),))],
        compiler_params=params(SMALL),
    )(*arrays)


def stack_body(first, second, out, sems):
    rows = first.shape[0]
    for copy in started([(first, out.at[:rows]), (second, out.at[rows:])], sems):
        copy.wait()


def stack(first, second):
    return pl.pallas_call(
        stack_body,
        out_shape=pltpu.VMEM((2 * first.shape[0], first.shape[1]), first.dtype),
        in_specs=[pl.BlockSpec(memory_space=pl.ANY)] * 2,
        out_specs=pl.BlockSpec(memory_space=pltpu.VMEM),
        scratch_shapes=[pltpu.SemaphoreType.DMA((2,))],
        compiler_params=params(SMALL),
    )(first, second)


def streamed_up_body(rows, kept, got, out, rows_held, kept_held, got_held, sems):
    hidden = kept.shape[1]
    bounds = tiles(rows.shape[1])
    pairs = []
    for low, high in bounds:
        span = slice(low, high)
        pairs.append((kept.at[span], kept_held.at[span]))
        pairs.append((got.at[span], got_held.at[span]))
        pairs.append((rows.at[:, span], rows_held.at[:, span]))
    copies = started(pairs, sems)
    for i, (low, high) in enumerate(bounds):
        for copy in copies[3 * i : 3 * i + 3]:
            copy.wait()
        piece = rows_held[:, low:high]
        mine = jnp.dot(piece, kept_held[low:high], preferred_element_type=F32)
        other = jnp.dot(piece, got_held[low:high], preferred_element_type=F32)
        if i == 0:
            out[:, :hidden] = mine
            out[:, hidden:] = other
        else:
            out[:, :hidden] += mine
            out[:, hidden:] += other


def up_body(rows, kept, got, out):
    hidden = kept.shape[1]
    out[:, :hidden] = jnp.dot(rows[...], kept[...], preferred_element_type=F32)
    out[:, hidden:] = jnp.dot(rows[...], got[...], preferred_element_type=F32)


def streamed_up(rows, kept, got):
    count, part = rows.shape
    return pl.pallas_call(
        streamed_up_body,
        out_shape=pltpu.VMEM((count, CORES * kept.shape[1]), F32),
        in_specs=[pl.BlockSpec(memory_space=pl.ANY)] * 3,
        out_specs=pl.BlockSpec(memory_space=pltpu.VMEM),
        scratch_shapes=[
            pltpu.VMEM(rows.shape, BF16),
            pltpu.VMEM(kept.shape, BF16),
            pltpu.VMEM(got.shape, BF16),
            pltpu.SemaphoreType.DMA((3 * len(tiles(part)),)),
        ],
        compiler_params=params(LARGE),
    )(rows, kept, got)


def up(rows, kept, got):
    return pl.pallas_call(
        up_body,
        out_shape=pltpu.VMEM((rows.shape[0], CORES * kept.shape[1]), F32),
        in_specs=[pl.BlockSpec(memory_space=pltpu.VMEM)] * 3,
        out_specs=pl.BlockSpec(memory_space=pltpu.VMEM),
        compiler_params=params(SMALL),
    )(rows, kept, got)


def down_body(mine, theirs, weight, out):
    hidden = weight.shape[0] // CORES
    first = jax.nn.silu(mine[:, :hidden] + theirs[:, hidden:]).astype(BF16)
    second = jax.nn.silu(mine[:, hidden:] + theirs[:, :hidden]).astype(BF16)
    active = jnp.concatenate([first, second], axis=1)
    for low, high in tiles(weight.shape[1]):
        total = jnp.dot(active, weight[:, low:high], preferred_element_type=F32)
        out[:, low:high] = total.astype(out.dtype)


def down(mine, theirs, weight):
    return pl.pallas_call(
        down_body,
        out_shape=jax.ShapeDtypeStruct((mine.shape[0], weight.shape[1]), BF16),
        in_specs=[pl.BlockSpec(memory_space=pltpu.VMEM)] * 3,
        out_specs=pl.BlockSpec(memory_space=pltpu.VMEM),
        compiler_params=params(SMALL),
    )(mine, theirs, weight)


def finish_body(capacity, moment, first, second, returned, routes, gates, *refs):
    outs, rest = refs[:COURSES], refs[COURSES:]
    news = rest[:COURSES] if rest else outs
    experts = returned.shape[0]
    part = returned.shape[-1]
    chosen = [column(routes[course, moment]) for course in range(COURSES)]
    tables = [tokens_by_slots(route, experts, capacity) for route in chosen]
    scales = [column(gates[course, moment]) for course in range(COURSES)]
    leaving = []
    for core in range(CORES):
        for low in range(0, part, TILE // 2):
            high = low + TILE // 2
            summed = [
                returned[e, 0, core, :, low:high].astype(F32)
                + returned[e, 1, core, :, low:high].astype(F32)
                for e in range(experts)
            ]
            columns = slice(core * part + low, core * part + high)
            for course, (state, new) in enumerate(((first, news[0]), (second, news[1]))):
                span = slice(course * capacity, (course + 1) * capacity)
                produced = jnp.concatenate([block[span] for block in summed], axis=0)
                gathered = jnp.dot(
                    tables[course], produced.astype(BF16), preferred_element_type=F32
                )
                new[:, columns] = (
                    state[:, columns].astype(F32) + gathered * scales[course]
                ).astype(BF16)
        if rest:
            span = slice(core * part, (core + 1) * part)
            for course in range(COURSES):
                copy = pltpu.make_async_copy(
                    news[course].at[:, span],
                    outs[course].at[:, span],
                    rest[COURSES].at[core, course],
                )
                copy.start()
                leaving.append(copy)
    for copy in leaving:
        copy.wait()


def finish(states, returned, routes, gates, experts, capacity, moment, last):
    tokens, width = states[0].shape
    rows, part = returned.shape[-2:]
    shape = (experts, HALVES, CORES, rows, part)
    vmem = pl.BlockSpec(memory_space=pltpu.VMEM)
    scratch = [pltpu.VMEM((tokens, width), BF16)] * COURSES
    scratch.append(pltpu.SemaphoreType.DMA((CORES, COURSES)))
    return pl.pallas_call(
        functools.partial(finish_body, capacity, moment),
        out_shape=[jax.ShapeDtypeStruct((tokens, width), BF16)] * COURSES,
        in_specs=[vmem] * 5,
        out_specs=[pl.BlockSpec(memory_space=pl.ANY) if last else vmem] * COURSES,
        scratch_shapes=scratch if last else [],
        compiler_params=params(SMALL),
    )(*states, returned.reshape(shape), routes, gates)


def per_device(
    forward_batch, reverse_batch, norm_gain, routes, gate_values, up_weight, down_weight
):
    devices = lax.axis_size("expert")
    experts = devices // SPLIT
    states = [forward_batch[0], reverse_batch[0]]
    tokens, width = states[0].shape
    capacity = tokens // experts
    part = width // CORES
    block = (devices, COURSES * capacity, part)

    core = lax.axis_index("expert") % CORES
    up_own, down_own = up_weight[0, 0], down_weight[0, 0]
    up_got = across_cores(lax.dynamic_slice_in_dim(up_own, (1 - core) * part, part, 0))
    down_got = across_cores(lax.dynamic_slice_in_dim(down_own, (1 - core) * part, part, 1))
    up_kept = lax.dynamic_slice_in_dim(up_own, core * part, part, 0)
    down_kept = lax.dynamic_slice_in_dim(down_own, core * part, part, 1)

    near_down = stack(down_kept, down_got)
    lines = (COURSES, STEPS, 1, tokens)
    routes, gates = routes.reshape(lines), gate_values.reshape(lines)
    for t in range(STEPS):
        limit = LARGE if t == 0 else SMALL
        sending = prepare(states, norm_gain, routes, experts, capacity, t, limit)
        rows = exchange(sending.reshape(block)).reshape(-1, part)
        rows, near_down = lax.optimization_barrier((rows, near_down))
        if t == 0:
            sums = streamed_up(rows, up_kept, up_got)
        else:
            sums = up(rows, *near_up)
        partial = down(sums, across_cores(sums), near_down)
        returned = exchange(partial.reshape(block))
        last = t + 1 == STEPS
        states = finish(states, returned, routes, gates, experts, capacity, t, last)
        if not last:
            up_kept, up_got, *states = lax.optimization_barrier((up_kept, up_got, *states))
            near_up = hold(up_kept, up_got)
            states = [passed_along(states[c], "section", 1 - 2 * c) for c in range(COURSES)]
            states, near_up = lax.optimization_barrier((states, near_up))
    return (states[0][None], states[1][None])


def solution(mesh):
    return jax.shard_map(
        per_device,
        mesh=mesh,
        in_specs=(
            P("section", "expert", None),
            P("section", "expert", None),
            P("section", None),
            P("section", None, None, "expert", None),
            P("section", None, None, "expert", None),
            P("section", "expert", None, None),
            P("section", "expert", None, None),
        ),
        out_specs=(P("section", "expert", None), P("section", "expert", None)),
        check_vma=False,
    )
```
